32 devices in a mesh: dp: 16 (over z, y, x), tensor: 2 (over core).
Axes of the slice: x: 2, y: 2, z: 4, core: 2. Of those that a mesh axis runs over, the one named last changes fastest.
Arguments:
- inputs: bfloat16 [6144, 12288], P('dp', 'tensor'), may hold values from -160 to 160
- out_grad: bfloat16 [6144, 6144], P('dp'), may hold values from -0.08930431 to 0.08930431
- weight_codes: bfloat16 [6144, 12288], P('dp', 'tensor'), may hold values from -1 to 1
- weight_scales: bfloat16 [6144], P('dp'), may hold values from 0.0039978027 to 0.019897461
- master: float32 [6144, 12288], P('dp', 'tensor'), may hold values from -0.8 to 0.8
- moment: float32 [6144, 12288], P('dp', 'tensor'), may hold values from -3 to 3
- second: float32 [6144, 12288], P('dp', 'tensor'), may hold values from 0.05 to 0.5
Outputs:
- grad_input: bfloat16 [6144, 12288], P('dp', 'tensor')
- new_master: float32 [6144, 12288], P('dp', 'tensor')
- new_moment: float32 [6144, 12288], P('dp', 'tensor')
- new_second: float32 [6144, 12288], P('dp', 'tensor')
- new_codes: bfloat16 [6144, 12288], P('dp', 'tensor')
- new_scales: bfloat16 [6144], P('dp')
- grad_peak: float32 [], replicated
The draws below stay inside these ranges and needn't reach their ends.
All inputs are finite; a program needn't handle non-finite values. Where the reference program divides by a largest or mean magnitude, that divisor is 1e-20 or more.
Results may differ from the reference program's by a relative error of at most 0.019.
Values may be sent and summed in bfloat16 or wider, within the bound.
A program may use at most 512 MiB of HBM per device.

```python
import math
import jax
import jax.numpy as jnp
from jax import lax

IN = 12288
OUT = 6144
TOK_DEV = 384
TOKENS = 6144
N_DP = 16


def rising(number):
    return jnp.power(3.0, jnp.arange(number, dtype=jnp.float32) / max(number - 1, 1))


def scaled_field(key, height, width, spread):
    normal_key = jax.random.fold_in(jax.random.fold_in(key, 11), 0)
    row_scale = rising(height)
    column_scale = rising(width)
    base = jnp.clip(jax.random.normal(normal_key, (height, width), jnp.float32), -4.0, 4.0)
    return spread * base * row_scale[:, None] * column_scale[None, :]


def draw_inputs(key, part):
    return scaled_field(key, TOKENS, IN, 1.0).astype(jnp.bfloat16)


def draw_out_grad(key, part):
    spread = 0.045 / TOKENS ** 0.5
    return scaled_field(jax.random.fold_in(key, 5), TOKENS, OUT, spread).astype(jnp.bfloat16)


def draw_master(key, part):
    normal_key = jax.random.fold_in(jax.random.fold_in(key, 7), 0)
    column_scale = rising(IN)
    base = jnp.clip(jax.random.normal(normal_key, (OUT, IN), jnp.float32), -4.0, 4.0)
    return 0.02 * base * column_scale[None, :]


def level_of(stream_key, shape, cuts, least, largest):
    factor_of = 1.0
    for dim, parts in cuts:
        steps = jax.random.uniform(jax.random.fold_in(jax.random.fold_in(stream_key, 6), dim), (parts,), jnp.float32, least / len(cuts), largest / len(cuts))
        factor_of = factor_of * jnp.repeat(jnp.exp(steps), shape[dim] // parts).reshape((-1,) + (1,) * (len(shape) - 1 - dim))
    return factor_of


def noise(key, dims, deviation, reach, cuts=(), kind=jnp.bfloat16):
    drawn = deviation * jax.random.normal(key, dims, jnp.float32)
    if cuts:
        drawn = drawn * level_of(key, dims, cuts, -0.22, 0.18)
    return jnp.clip(drawn, -reach, reach).astype(kind)


def setup_inputs(seed: int = 0) -> dict:
    arg_keys = jax.random.split(jax.random.key(seed), 8)
    return {
        "inputs": draw_inputs(jax.random.fold_in(arg_keys[7], 71), 0),
        "out_grad": draw_out_grad(jax.random.fold_in(arg_keys[7], 71), 0),
        "weight_codes": jnp.clip(jax.random.uniform(arg_keys[2], (OUT, IN), jnp.float32, -1.0, 1.0) * level_of(arg_keys[2], (OUT, IN), ((0, 16), (1, 2)), -0.4, 0.0), -1.0, 1.0).astype(jnp.bfloat16),
        "weight_scales": jnp.clip(jnp.exp(math.log(0.019897461) - 1.6048472 * jax.random.uniform(arg_keys[3], (OUT,), jnp.float32) ** level_of(arg_keys[3], (OUT,), ((0, 16),), -0.2, 0.2)), 0.0039978027, 0.019897461).astype(jnp.bfloat16),
        "master": draw_master(jax.random.fold_in(arg_keys[7], 71), 0),
        "moment": noise(arg_keys[5], (OUT, IN), 0.5, 3.0, ((0, 16), (1, 2)), jnp.float32),
        "second": jnp.clip(jnp.exp(math.log(0.5) - 2.3025851 * jax.random.uniform(arg_keys[6], (OUT, IN), jnp.float32) ** level_of(arg_keys[6], (OUT, IN), ((0, 16), (1, 2)), -0.2, 0.2)), 0.05, 0.5),
    }


def block_term(grads, acts):
    return lax.dot_general(grads, acts, (((0,), (0,)), ((), ())), preferred_element_type=jnp.float32)

def grid_round(partial_value, divisor):
    scaled = lax.optimization_barrier((partial_value / divisor * 64.0).astype(jnp.bfloat16))
    return scaled.astype(jnp.float32)

def reference(inputs, out_grad, weight_codes, weight_scales, master, moment, second):
    weight = (weight_codes.astype(jnp.float32) * weight_scales.astype(jnp.float32)[:, None]).astype(jnp.bfloat16)
    grad_input = jnp.dot(out_grad, weight, preferred_element_type=jnp.float32).astype(jnp.bfloat16)
    acts_blocks = inputs.reshape(N_DP, TOK_DEV, IN)
    grad_blocks = out_grad.reshape(N_DP, TOK_DEV, OUT)

    def peak_step(carry, pair):
        return (jnp.maximum(carry, jnp.max(jnp.abs(block_term(pair[0], pair[1])))), None)
    grad_peak = lax.scan(peak_step, jnp.zeros((), jnp.float32), (grad_blocks, acts_blocks))[0]
    divisor = grad_peak + 1e-06

    def sum_step(carry, pair):
        return (carry + grid_round(block_term(pair[0], pair[1]), divisor), None)
    summed = lax.scan(sum_step, jnp.zeros((OUT, IN), jnp.float32), (grad_blocks, acts_blocks))[0]
    gradient = summed * divisor / 64.0
    total_norm = jnp.sqrt(jnp.sum(gradient * gradient))
    clip_factor = jnp.minimum(1.0, jnp.sqrt(jnp.float32(OUT * IN)) / (total_norm + 1e-06))
    clipped = clip_factor * gradient
    new_moment = 0.9 * moment + 0.1 * clipped
    new_second = 0.95 * second + 0.05 * clipped * clipped
    new_master = master - 0.01 * (new_moment / (jnp.sqrt(new_second) + 1e-08) + 0.1 * master)
    row_peak = lax.optimization_barrier(jnp.max(jnp.abs(new_master), axis=1)) + 1e-06
    new_codes = (new_master / row_peak[:, None]).astype(jnp.bfloat16)
    new_scales = row_peak.astype(jnp.bfloat16)
    return (grad_input, new_master, new_moment, new_second, new_codes, new_scales, grad_peak)
```

```python
import math

import jax
import jax.numpy as jnp
from jax import lax
from jax.sharding import PartitionSpec as P


def inner_size(n):
    for size in range(math.isqrt(n), 0, -1):
        if n % size == 0:
            return n // size
    return n


def on_device(n, inputs, out_grad, weight_codes, weight_scales, master, moment, second):
    inner = inner_size(n)
    outer = n // inner
    lines_of = [[a * inner + b for a in range(outer)] for b in range(inner)]
    tok = inputs.shape[0]
    own = weight_codes.shape[0]
    cols = inputs.shape[1]
    place = lax.rem(lax.axis_index("dp"), inner)
    paired = inner & (inner - 1) == 0

    def partner(b, step):
        return b ^ step if paired else (inner + step - b) % inner

    def swap(value, step):
        pairs = [(a * inner + b, a * inner + partner(b, step)) for a in range(outer) for b in range(inner)]
        return lax.ppermute(value, "dp", pairs)

    def moves(step):
        return step > 0 or not paired

    weight = (weight_codes.astype(jnp.float32) * weight_scales.astype(jnp.float32)[:, None]).astype(jnp.bfloat16)
    weight = lax.all_gather(weight, "dp", axis=0, tiled=True, axis_index_groups=lines_of)

    blocks = out_grad.reshape(tok, outer, inner, own).transpose(2, 0, 1, 3).reshape(inner, tok, outer * own)
    grads = []
    acts = []
    for step in range(inner):
        block = lax.dynamic_index_in_dim(blocks, partner(place, step), 0, keepdims=False)
        grads.append(swap(block, step) if moves(step) else block)
    for step in range(inner):
        acts.append(swap(inputs, step) if moves(step) else inputs)

    total = None
    peak = None
    for block, act in zip(grads, acts):
        term = lax.dot_general(
            block, act, (((0,), (0,)), ((), ())), preferred_element_type=jnp.float32
        )
        high = jnp.max(jnp.abs(term))
        total = term if total is None else total + term
        peak = high if peak is None else jnp.maximum(peak, high)
    summed = lax.psum_scatter(
        total.astype(jnp.bfloat16), "dp", scatter_dimension=0, tiled=True, axis_index_groups=lines_of
    )
    grad_peak = lax.pmax(peak, ("dp", "tensor"))
    weight, grad_peak = lax.optimization_barrier((weight, grad_peak))

    grad_input = None
    for step in range(inner):
        folded = jnp.dot(grads[step], weight, preferred_element_type=jnp.float32)
        if moves(step):
            folded = swap(folded.astype(jnp.bfloat16), step).astype(jnp.float32)
        grad_input = folded if grad_input is None else grad_input + folded
    grad_input = grad_input.astype(jnp.bfloat16)

    gradient = summed.astype(jnp.float32)
    squares = lax.psum(jnp.sum(gradient * gradient), ("dp", "tensor"))
    entries = jnp.float32(own * n * cols * lax.axis_size("tensor"))
    clip_factor = jnp.minimum(1.0, jnp.sqrt(entries) / (jnp.sqrt(squares) + 1e-06))
    clipped = clip_factor * gradient
    new_moment = 0.9 * moment + 0.1 * clipped
    new_second = 0.95 * second + 0.05 * clipped * clipped
    new_master = master - 0.01 * (new_moment / (jnp.sqrt(new_second) + 1e-08) + 0.1 * master)
    row_peak = lax.pmax(jnp.max(jnp.abs(new_master), axis=1), "tensor") + 1e-06
    new_codes = (new_master / row_peak[:, None]).astype(jnp.bfloat16)
    new_scales = row_peak.astype(jnp.bfloat16)
    return (grad_input, new_master, new_moment, new_second, new_codes, new_scales, grad_peak)


def solution(mesh):
    n = mesh.shape["dp"]

    def body(*args):
        return on_device(n, *args)

    return jax.shard_map(
        body,
        mesh=mesh,
        in_specs=(
            P("dp", "tensor"),
            P("dp", None),
            P("dp", "tensor"),
            P("dp"),
            P("dp", "tensor"),
            P("dp", "tensor"),
            P("dp", "tensor"),
        ),
        out_specs=(
            P("dp", "tensor"),
            P("dp", "tensor"),
            P("dp", "tensor"),
            P("dp", "tensor"),
            P("dp", "tensor"),
            P("dp"),
            P(),
        ),
        check_vma=False,
    )
```

```python
import math

import jax
import jax.numpy as jnp
from jax import lax
from jax.sharding import PartitionSpec as P


def inner_size(n):
    for size in range(math.isqrt(n), 0, -1):
        if n % size == 0:
            return n // size
    return n


def on_device(n, inputs, out_grad, weight_codes, weight_scales, master, moment, second):
    inner = inner_size(n)
    outer = n // inner
    lines_of = [[a * inner + b for a in range(outer)] for b in range(inner)]
    tok = inputs.shape[0]
    own = weight_codes.shape[0]
    cols = inputs.shape[1]
    place = lax.rem(lax.axis_index("dp"), inner)
    paired = inner & (inner - 1) == 0

    def partner(b, step):
        return b ^ step if paired else (inner + step - b) % inner

    def swap(value, step):
        pairs = [(a * inner + b, a * inner + partner(b, step)) for a in range(outer) for b in range(inner)]
        return lax.ppermute(value, "dp", pairs)

    def moves(step):
        return step > 0 or not paired

    weight = (weight_codes.astype(jnp.float32) * weight_scales.astype(jnp.float32)[:, None]).astype(jnp.bfloat16)
    weight = lax.all_gather(weight, "dp", axis=0, tiled=True, axis_index_groups=lines_of)

    blocks = out_grad.reshape(tok, outer, inner, own).transpose(2, 0, 1, 3).reshape(inner, tok, outer * own)
    grads = []
    acts = []
    for step in range(inner):
        block = lax.dynamic_index_in_dim(blocks, partner(place, step), 0, keepdims=False)
        grads.append(swap(block, step) if moves(step) else block)
    for step in range(inner):
        acts.append(swap(inputs, step) if moves(step) else inputs)

    total = None
    peak = None
    for block, act in zip(grads, acts):
        term = lax.dot_general(
            block, act, (((0,), (0,)), ((), ())), preferred_element_type=jnp.float32
        )
        high = jnp.max(jnp.abs(term))
        total = term if total is None else total + term
        peak = high if peak is None else jnp.maximum(peak, high)
    summed = lax.psum_scatter(
        total.astype(jnp.bfloat16), "dp", scatter_dimension=0, tiled=True, axis_index_groups=lines_of
    )
    grad_peak = lax.pmax(peak, ("dp", "tensor"))
    weight, grad_peak = lax.optimization_barrier((weight, grad_peak))

    grad_input = None
    for step in range(inner):
        folded = jnp.dot(grads[step], weight, preferred_element_type=jnp.float32)
        if moves(step):
            folded = swap(folded.astype(jnp.bfloat16), step).astype(jnp.float32)
        grad_input = folded if grad_input is None else grad_input + folded
    grad_input = grad_input.astype(jnp.bfloat16)

    gradient = summed.astype(jnp.float32)
    squares = lax.psum(jnp.sum(gradient * gradient), "tensor")
    if n & (n - 1) == 0:
        for bit in range(n.bit_length() - 1):
            squares += lax.ppermute(squares, "dp", [(i, i ^ (1 << bit)) for i in range(n)])
    else:
        squares = lax.psum(squares, "dp")
    entries = jnp.float32(own * n * cols * lax.axis_size("tensor"))
    clip_factor = jnp.minimum(1.0, jnp.sqrt(entries) / (jnp.sqrt(squares) + 1e-06))
    clipped = clip_factor * gradient
    new_moment = 0.9 * moment + 0.1 * clipped
    new_second = 0.95 * second + 0.05 * clipped * clipped
    new_master = master - 0.01 * (new_moment / (jnp.sqrt(new_second) + 1e-08) + 0.1 * master)
    row_peak = lax.pmax(jnp.max(jnp.abs(new_master), axis=1), "tensor") + 1e-06
    new_codes = (new_master / row_peak[:, None]).astype(jnp.bfloat16)
    new_scales = row_peak.astype(jnp.bfloat16)
    return (grad_input, new_master, new_moment, new_second, new_codes, new_scales, grad_peak)


def solution(mesh):
    n = mesh.shape["dp"]

    def body(*args):
        return on_device(n, *args)

    return jax.shard_map(
        body,
        mesh=mesh,
        in_specs=(
            P("dp", "tensor"),
            P("dp", None),
            P("dp", "tensor"),
            P("dp"),
            P("dp", "tensor"),
            P("dp", "tensor"),
            P("dp", "tensor"),
        ),
        out_specs=(
            P("dp", "tensor"),
            P("dp", "tensor"),
            P("dp", "tensor"),
            P("dp", "tensor"),
            P("dp", "tensor"),
            P("dp"),
            P(),
        ),
        check_vma=False,
    )
```
